256 devices in a mesh: seq: 32 (over y, z), head: 8 (over x, core).
Axes of the slice: x: 4, y: 4, z: 8, core: 2. Of those that a mesh axis runs over, the one named last changes fastest.
Arguments:
- queries: bfloat16 [32768, 32, 128], P('seq', 'head'), may hold values from -6 to 6
- key_rows: bfloat16 [32768, 32, 128], P('seq', 'head'), may hold values from -6 to 6
- value_rows: bfloat16 [32768, 32, 128], P('seq', 'head'), may hold values from -6 to 6
- out_grad: bfloat16 [32768, 4096], P('seq', 'head'), may hold values from -6 to 6
- out_weight: bfloat16 [32, 128, 4096], P('head'), may hold values from -0.09375 to 0.09375
Outputs:
- query_grad: bfloat16 [32768, 32, 128], P('seq', 'head')
- key_grad: bfloat16 [32768, 32, 128], P('seq', 'head')
- value_grad: bfloat16 [32768, 32, 128], P('seq', 'head')
The draws below stay inside these ranges and needn't reach their ends.
All inputs are finite; a program needn't handle non-finite values.
Results may differ from the reference program's by a relative error of at most 0.0058.
Values may be sent and summed in bfloat16 or wider, within the bound.
No kernel may reach another device: no remote copies, remote signals or barrier semaphores. Data moves between devices by JAX's collectives and lax.ppermute only.
A program may use at most 128 MiB of HBM per device.

```python
import math
import jax
import jax.numpy as jnp
from jax import lax

D = 4096
HEADS = 32
DH = 128
BLOCK = 256
TOKENS = 32768


def shard_levels(key, extent, split, least, high):
    factor_of = 1.0
    for position, blocks in split:
        steps = jax.random.uniform(jax.random.fold_in(jax.random.fold_in(key, 6), position), (blocks,), jnp.float32, least / len(split), high / len(split))
        factor_of = factor_of * jnp.repeat(jnp.exp(steps), extent[position] // blocks).reshape((-1,) + (1,) * (len(extent) - 1 - position))
    return factor_of


def noise(stream_key, dims, deviation, bound, shards=(), dtype=jnp.bfloat16):
    array = deviation * jax.random.normal(stream_key, dims, jnp.float32)
    if shards:
        array = array * shard_levels(stream_key, dims, shards, -0.22, 0.18)
    return jnp.clip(array, -bound, bound).astype(dtype)


def setup_inputs(seed: int = 0) -> dict:
    arg_keys = jax.random.split(jax.random.key(seed), 6)
    queries = noise(arg_keys[0], (TOKENS, HEADS, DH), 1.0, 6.0, ((0, 32), (1, 8)))
    key_rows = noise(arg_keys[1], (TOKENS, HEADS, DH), 1.0, 6.0, ((0, 32), (1, 8)))
    value_rows = noise(arg_keys[2], (TOKENS, HEADS, DH), 1.0, 6.0, ((0, 32), (1, 8)))
    out_grad = noise(arg_keys[3], (TOKENS, D), 1.0, 6.0, ((0, 32), (1, 8)))
    out_weight = noise(arg_keys[4], (HEADS, DH, D), D ** -0.5, 0.09375, ((0, 8),))
    return {"queries": queries, "key_rows": key_rows, "value_rows": value_rows, "out_grad": out_grad, "out_weight": out_weight}


def round_bf(values):
    return lax.optimization_barrier(values.astype(jnp.bfloat16)).astype(jnp.float32)

def one_head(arrays):
    query_head, key_head, value_head, grad_head = arrays
    count = TOKENS // BLOCK
    query_blocks = query_head.reshape(count, BLOCK, DH).astype(jnp.float32)
    key_blocks = key_head.reshape(count, BLOCK, DH).astype(jnp.float32)
    value_blocks = value_head.reshape(count, BLOCK, DH).astype(jnp.float32)
    grad_blocks = grad_head.reshape(count, BLOCK, DH).astype(jnp.float32)
    kv_parts = jnp.einsum('btd,bte->bde', key_blocks, value_blocks)
    qg_parts = jnp.einsum('btd,bte->bde', query_blocks, grad_blocks)
    zero_state = jnp.zeros((1, DH, DH), jnp.float32)
    prefix = jnp.concatenate([zero_state, jnp.cumsum(kv_parts, 0)[:-1]], 0)
    backward_sums = jnp.cumsum(qg_parts[::-1], 0)[::-1]
    suffix = jnp.concatenate([backward_sums[1:], zero_state], 0)
    prefix_bf = round_bf(prefix)
    suffix_bf = round_bf(suffix)
    causal = jnp.tril(jnp.ones((BLOCK, BLOCK), bool))
    qk_scores = round_bf(jnp.where(causal, jnp.einsum('btd,bsd->bts', query_blocks, key_blocks), 0.0))
    grad_scores = round_bf(jnp.where(causal, jnp.einsum('btd,bsd->bts', grad_blocks, value_blocks), 0.0))
    factor = 1.0 / math.sqrt(DH * TOKENS)
    query_grad = jnp.einsum('bts,bsd->btd', grad_scores, key_blocks) + jnp.einsum('bte,bde->btd', grad_blocks, prefix_bf)
    key_grad = jnp.einsum('bts,btd->bsd', grad_scores, query_blocks) + jnp.einsum('bse,bde->bsd', value_blocks, suffix_bf)
    value_grad = jnp.einsum('bts,bte->bse', qk_scores, grad_blocks) + jnp.einsum('bsd,bde->bse', key_blocks, suffix_bf)
    return ((factor * query_grad).astype(jnp.bfloat16).reshape(TOKENS, DH), (factor * key_grad).astype(jnp.bfloat16).reshape(TOKENS, DH), (factor * value_grad).astype(jnp.bfloat16).reshape(TOKENS, DH))

def reference(queries, key_rows, value_rows, out_grad, out_weight):
    weight = out_weight.reshape(HEADS * DH, D).astype(jnp.float32)
    attn_grad = jnp.dot(out_grad.astype(jnp.float32), weight.T, preferred_element_type=jnp.float32)
    attn_grad = attn_grad.astype(jnp.bfloat16).reshape(TOKENS, HEADS, DH)
    stacked = (queries.transpose(1, 0, 2), key_rows.transpose(1, 0, 2), value_rows.transpose(1, 0, 2), attn_grad.transpose(1, 0, 2))
    query_grad, key_grad, value_grad = lax.map(one_head, stacked)
    return (query_grad.transpose(1, 0, 2), key_grad.transpose(1, 0, 2), value_grad.transpose(1, 0, 2))
```

```python
import math

import jax
import jax.numpy as jnp
from jax import lax
from jax.experimental import pallas as pl
from jax.experimental.pallas import tpu as pltpu
from jax.sharding import PartitionSpec as P

BLOCK = 256
F32 = jnp.float32
BF16 = jnp.bfloat16


def dot(a, b, ca, cb):
    return lax.dot_general(a, b, (((ca,), (cb,)), ((), ())), preferred_element_type=F32)


def params(mib=40):
    return pltpu.CompilerParams(vmem_limit_bytes=mib * 1024 * 1024)


def kv_kernel(heads, k_ref, v_ref, before_ref, total_ref, run):
    step = pl.program_id(0)

    @pl.when(step == 0)
    def _():
        run[...] = jnp.zeros_like(run)

    before_ref[0] = run[...]
    for h in range(heads):
        run[h] += dot(k_ref[h], v_ref[h], 0, 0)
    total_ref[...] = run[...].astype(BF16)


def kv_states(k, v):
    heads, tokens, depth = k.shape
    blocks = tokens // BLOCK
    spec = pl.BlockSpec((heads, BLOCK, depth), lambda b: (0, b, 0))
    return pl.pallas_call(
        lambda *refs: kv_kernel(heads, *refs),
        grid=(blocks,),
        in_specs=[spec, spec],
        out_specs=[
            pl.BlockSpec((1, heads, depth, depth), lambda b: (b, 0, 0, 0)),
            pl.BlockSpec((heads, depth, depth), lambda b: (0, 0, 0)),
        ],
        out_shape=[
            jax.ShapeDtypeStruct((blocks, heads, depth, depth), F32),
            jax.ShapeDtypeStruct((heads, depth, depth), BF16),
        ],
        scratch_shapes=[pltpu.VMEM((heads, depth, depth), F32)],
        compiler_params=params(),
        name="kv_states",
    )(k, v)


def attn_first_kernel(width, index_ref, *refs):
    pieces, w_ref, acc_ref = refs[:-2], refs[-2], refs[-1]
    total = None
    for i, piece in enumerate(pieces):
        start = pl.multiple_of(index_ref[i] * width, 128)
        part = dot(piece[...], w_ref[:, pl.ds(start, width)], 1, 1)
        total = part if total is None else total + part
    acc_ref[...] = total


def attn_first(pieces, index, w):
    tokens, width = pieces[0].shape
    rows = w.shape[0]
    spec = pl.BlockSpec((BLOCK, width), lambda b, i: (b, 0))
    return pl.pallas_call(
        lambda *refs: attn_first_kernel(width, *refs),
        grid_spec=pltpu.PrefetchScalarGridSpec(
            num_scalar_prefetch=1,
            grid=(tokens // BLOCK,),
            in_specs=[spec] * len(pieces) + [pl.BlockSpec(w.shape, lambda b, i: (0, 0))],
            out_specs=pl.BlockSpec((BLOCK, rows), lambda b, i: (b, 0)),
        ),
        out_shape=jax.ShapeDtypeStruct((tokens, rows), F32),
        compiler_params=params(),
        name="attn_first",
    )(index, *pieces, w)


def attn_last_kernel(heads, index_ref, a_ref, b_ref, wa_ref, wb_ref, acc_ref, qt_ref, g_ref, after_ref, total_ref, run):
    step = pl.program_id(0)
    depth = qt_ref.shape[1]

    @pl.when(step == 0)
    def _():
        run[...] = jnp.zeros_like(run)

    total = acc_ref[...] + dot(a_ref[...], wa_ref[...], 1, 1)
    total = (total + dot(b_ref[...], wb_ref[...], 1, 1)).astype(BF16)
    g_ref[...] = total
    after_ref[0] = run[...]
    for h in range(heads):
        run[h] += dot(qt_ref[h], total[:, h * depth : (h + 1) * depth], 1, 0)
    total_ref[...] = run[...].astype(BF16)


def attn_last(a, b, index, w, acc, qt):
    tokens, width = a.shape
    rows = w.shape[0]
    heads, depth, _ = qt.shape
    blocks = tokens // BLOCK
    last = blocks - 1
    piece = pl.BlockSpec((BLOCK, width), lambda s, i: (last - s, 0))
    wide = pl.BlockSpec((BLOCK, rows), lambda s, i: (last - s, 0))
    return pl.pallas_call(
        lambda *refs: attn_last_kernel(heads, *refs),
        grid_spec=pltpu.PrefetchScalarGridSpec(
            num_scalar_prefetch=1,
            grid=(blocks,),
            in_specs=[
                piece,
                piece,
                pl.BlockSpec((rows, width), lambda s, i: (0, i[0])),
                pl.BlockSpec((rows, width), lambda s, i: (0, i[1])),
                wide,
                pl.BlockSpec((heads, depth, BLOCK), lambda s, i: (0, 0, last - s)),
            ],
            out_specs=[
                wide,
                pl.BlockSpec((1, heads, depth, depth), lambda s, i: (last - s, 0, 0, 0)),
                pl.BlockSpec((heads, depth, depth), lambda s, i: (0, 0, 0)),
            ],
            scratch_shapes=[pltpu.VMEM((heads, depth, depth), F32)],
        ),
        out_shape=[
            jax.ShapeDtypeStruct((tokens, rows), BF16),
            jax.ShapeDtypeStruct((blocks, heads, depth, depth), F32),
            jax.ShapeDtypeStruct((heads, depth, depth), BF16),
        ],
        compiler_params=params(),
        name="attn_last",
    )(index, a, b, w, w, acc, qt)


def inner_kernel(heads, q_ref, k_ref, v_ref, g_ref, qi_ref, ki_ref, vi_ref):
    depth = q_ref.shape[2]
    row = lax.broadcasted_iota(jnp.int32, (BLOCK, BLOCK), 0)
    col = lax.broadcasted_iota(jnp.int32, (BLOCK, BLOCK), 1)
    for h in range(heads):
        lanes = slice(h * depth, (h + 1) * depth)
        q, k, v, g = q_ref[h], k_ref[h], v_ref[h], g_ref[:, lanes]
        grad = jnp.where(col <= row, dot(g, v, 1, 1), 0.0).astype(BF16)
        grad_t = jnp.where(row <= col, dot(v, g, 1, 1), 0.0).astype(BF16)
        score_t = jnp.where(row <= col, dot(k, q, 1, 1), 0.0).astype(BF16)
        qi_ref[:, lanes] = dot(grad, k, 1, 0)
        ki_ref[:, lanes] = dot(grad_t, q, 1, 0)
        vi_ref[:, lanes] = dot(score_t, g, 1, 0)


def inner(q, k, v, g):
    heads, tokens, depth = q.shape
    rows = heads * depth
    split = pl.BlockSpec((heads, BLOCK, depth), lambda b: (0, b, 0))
    wide = pl.BlockSpec((BLOCK, rows), lambda b: (b, 0))
    return pl.pallas_call(
        lambda *refs: inner_kernel(heads, *refs),
        grid=(tokens // BLOCK,),
        in_specs=[split, split, split, wide],
        out_specs=[wide] * 3,
        out_shape=[jax.ShapeDtypeStruct((tokens, rows), F32)] * 3,
        compiler_params=params(),
        name="inner",
    )(q, k, v, g)


def query_kernel(heads, factor, g_ref, qi_ref, local_ref, far_ref, out_ref, flat):
    depth = far_ref.shape[1]
    for h in range(heads):
        lanes = slice(h * depth, (h + 1) * depth)
        state = (far_ref[h].astype(F32) + local_ref[0, h]).astype(BF16)
        flat[:, h, :] = factor * (qi_ref[:, lanes] + dot(g_ref[:, lanes], state, 1, 1))
    out_ref[...] = flat[...].astype(BF16)


def query_out(g, qi, local, far, factor):
    tokens, rows = g.shape
    heads, depth, _ = far.shape
    wide = pl.BlockSpec((BLOCK, rows), lambda b: (b, 0))
    return pl.pallas_call(
        lambda *refs: query_kernel(heads, factor, *refs),
        grid=(tokens // BLOCK,),
        in_specs=[
            wide,
            wide,
            pl.BlockSpec((1, heads, depth, depth), lambda b: (b, 0, 0, 0)),
            pl.BlockSpec((heads, depth, depth), lambda b: (0, 0, 0)),
        ],
        out_specs=pl.BlockSpec((BLOCK, heads, depth), lambda b: (b, 0, 0)),
        out_shape=jax.ShapeDtypeStruct((tokens, heads, depth), BF16),
        scratch_shapes=[pltpu.VMEM((BLOCK, heads, depth), F32)],
        compiler_params=params(),
        name="query_out",
    )(g, qi, local, far)


def key_value_kernel(heads, factor, k_ref, v_ref, ki_ref, vi_ref, local_ref, far_ref, ko_ref, vo_ref, kf, vf):
    depth = far_ref.shape[1]
    for h in range(heads):
        lanes = slice(h * depth, (h + 1) * depth)
        state = (far_ref[h].astype(F32) + local_ref[0, h]).astype(BF16)
        kf[:, h, :] = factor * (ki_ref[:, lanes] + dot(v_ref[h], state, 1, 1))
        vf[:, h, :] = factor * (vi_ref[:, lanes] + dot(k_ref[h], state, 1, 0))
    ko_ref[...] = kf[...].astype(BF16)
    vo_ref[...] = vf[...].astype(BF16)


def key_value_out(k, v, ki, vi, local, far, factor):
    tokens, rows = ki.shape
    heads, depth, _ = far.shape
    split = pl.BlockSpec((heads, BLOCK, depth), lambda b: (0, b, 0))
    wide = pl.BlockSpec((BLOCK, rows), lambda b: (b, 0))
    out = pl.BlockSpec((BLOCK, heads, depth), lambda b: (b, 0, 0))
    return pl.pallas_call(
        lambda *refs: key_value_kernel(heads, factor, *refs),
        grid=(tokens // BLOCK,),
        in_specs=[
            split,
            split,
            wide,
            wide,
            pl.BlockSpec((1, heads, depth, depth), lambda b: (b, 0, 0, 0)),
            pl.BlockSpec((heads, depth, depth), lambda b: (0, 0, 0)),
        ],
        out_specs=[out, out],
        out_shape=[jax.ShapeDtypeStruct((tokens, heads, depth), BF16)] * 2,
        scratch_shapes=[pltpu.VMEM((BLOCK, heads, depth), F32)] * 2,
        compiler_params=params(),
        name="key_value_out",
    )(k, v, ki, vi, local, far)


def body(queries, key_rows, value_rows, out_grad, out_weight):
    tokens, heads, depth = queries.shape
    shards = lax.axis_size("seq")
    columns = lax.axis_size("head")
    chips = columns // 2
    factor = 1.0 / math.sqrt(depth * tokens * shards)

    def along(shift):
        return [(2 * x + c, 2 * ((x + shift) % chips) + c) for x in range(chips) for c in range(2)]

    def send(array, pairs):
        return lax.ppermute(array, "head", pairs)

    swap = [(i, i ^ 1) for i in range(columns)]
    right, left = along(1), along(-1)
    half = tokens // 2
    from_left = send(out_grad, right)
    from_right = send(out_grad, left)
    twin = send(out_grad, swap)
    far_top = send(from_left[:half], right)
    far_bottom = send(from_right[half:], left)
    from_left_twin = send(from_left, swap)
    from_right_twin = send(from_right, swap)
    far_top_twin = send(far_top, swap)
    far_bottom_twin = send(far_bottom, swap)

    me = lax.axis_index("head")
    chip, core = me // 2, me % 2

    def column(shift, other):
        return 2 * ((chip + shift) % chips) + (1 - core if other else core)

    w = out_weight.reshape(heads * depth, -1)

    q = queries.transpose(1, 0, 2)
    k = key_rows.transpose(1, 0, 2)
    v = value_rows.transpose(1, 0, 2)
    qt = queries.transpose(1, 2, 0)

    kv_local, kv_total = kv_states(k, v)
    rows = heads * depth // shards
    kv_pieces = lax.all_to_all(kv_total.reshape(shards, rows, depth), "seq", 0, 0, tiled=True)
    earlier = jnp.tril(jnp.ones((shards, shards), BF16), -1)
    later = jnp.triu(jnp.ones((shards, shards), BF16), 1)

    def scan(mask, pieces):
        sums = dot(mask, pieces.reshape(shards, rows * depth), 1, 0)
        return sums.astype(BF16).reshape(shards, rows, depth)

    kv_sums = scan(earlier, kv_pieces)

    index = jnp.stack(
        [column(0, 0), column(0, 1), column(-1, 0), column(-1, 1), column(1, 0), column(1, 1)]
    ).astype(jnp.int32)
    acc = attn_first(
        [out_grad, twin, from_left, from_left_twin, from_right, from_right_twin], index, w
    )
    far = jnp.concatenate([far_top, far_bottom], 0)
    far_twin = jnp.concatenate([far_top_twin, far_bottom_twin], 0)
    far_index = jnp.stack([column(2, 0), column(2, 1)]).astype(jnp.int32)
    grad, qg_local, qg_total = attn_last(far, far_twin, far_index, w, acc, qt)

    both = jnp.concatenate([qg_total.reshape(shards, rows, depth), kv_sums], 1)
    both = lax.all_to_all(both, "seq", 0, 0, tiled=True)
    qg_sums = scan(later, both[:, :rows])
    before = both[:, rows:].reshape(heads, depth, depth)
    after = lax.all_to_all(qg_sums, "seq", 0, 0, tiled=True).reshape(heads, depth, depth)

    qi, ki, vi = inner(q, k, v, grad)
    query_grad = query_out(grad, qi, kv_local, before, factor)
    key_grad, value_grad = key_value_out(k, v, ki, vi, qg_local, after, factor)
    return query_grad, key_grad, value_grad


def solution(mesh):
    placed = (
        P("seq", "head", None),
        P("seq", "head", None),
        P("seq", "head", None),
        P("seq", "head"),
        P("head", None, None),
    )
    return jax.shard_map(
        body,
        mesh=mesh,
        in_specs=placed,
        out_specs=(P("seq", "head", None), P("seq", "head", None), P("seq", "head", None)),
        check_vma=False,
    )
```

```python
import math

import jax
import jax.numpy as jnp
from jax import lax
from jax.experimental import pallas as pl
from jax.experimental.pallas import tpu as pltpu
from jax.sharding import PartitionSpec as P

BLOCK = 256
STEP = 512
F32 = jnp.float32
BF16 = jnp.bfloat16


def dot(a, b, ca, cb):
    return lax.dot_general(a, b, (((ca,), (cb,)), ((), ())), preferred_element_type=F32)


def params(mib):
    return pltpu.CompilerParams(vmem_limit_bytes=mib * 1024 * 1024)


def in_hbm(array):
    return pltpu.with_memory_space_constraint(array, pltpu.HBM)


def cost(flops, moved):
    return pl.CostEstimate(flops=flops, bytes_accessed=moved, transcendentals=0)


def kv_kernel(heads, k_ref, v_ref, before_ref, total_ref, run):
    step = pl.program_id(0)

    @pl.when(step == 0)
    def _():
        run[...] = jnp.zeros_like(run)

    before_ref[0] = run[...]
    for h in range(heads):
        run[h] += dot(k_ref[h], v_ref[h], 0, 0)
    total_ref[...] = run[...].astype(BF16)


def kv_states(k, v):
    heads, tokens, depth = k.shape
    blocks = tokens // BLOCK
    spec = pl.BlockSpec((heads, BLOCK, depth), lambda b: (0, b, 0))
    return pl.pallas_call(
        lambda *refs: kv_kernel(heads, *refs),
        grid=(blocks,),
        in_specs=[spec, spec],
        out_specs=[
            pl.BlockSpec((1, heads, depth, depth), lambda b: (b, 0, 0, 0)),
            pl.BlockSpec((heads, depth, depth), lambda b: (0, 0, 0)),
        ],
        out_shape=[
            pltpu.HBM((blocks, heads, depth, depth), F32),
            jax.ShapeDtypeStruct((heads, depth, depth), BF16),
        ],
        scratch_shapes=[pltpu.VMEM((heads, depth, depth), F32)],
        compiler_params=params(6),
        name="kv_states",
    )(k, v)


def attn_add_kernel(count, acc_ref, *refs):
    total = None if acc_ref is None else acc_ref[...]
    for i in range(count):
        part = dot(refs[i][...], refs[count + i][...], 1, 1)
        total = part if total is None else total + part
    refs[-1][...] = total


def attn_add(acc, pieces, index, w, name):
    tokens, width = pieces[0].shape
    rows = w.shape[0]
    count = len(pieces)
    spec = pl.BlockSpec((BLOCK, width), lambda b, i: (b, 0))
    wide = pl.BlockSpec((BLOCK, rows), lambda b, i: (b, 0))
    weights = [pl.BlockSpec((rows, width), lambda b, i, j=j: (0, i[j])) for j in range(count)]
    first = [] if acc is None else [acc]
    return pl.pallas_call(
        lambda i, *refs: attn_add_kernel(count, *(refs if first else (None, *refs))),
        grid_spec=pltpu.PrefetchScalarGridSpec(
            num_scalar_prefetch=1,
            grid=(tokens // BLOCK,),
            in_specs=[wide] * len(first) + [spec] * count + weights,
            out_specs=wide,
        ),
        out_shape=jax.ShapeDtypeStruct((tokens, rows), F32),
        compiler_params=params(6 + 3 * count),
        cost_estimate=cost(2 * tokens * rows * width * count, 4 * tokens * rows),
        name=name,
    )(index, *first, *pieces, *([w] * count))


def attn_last_kernel(heads, i_ref, a_ref, b_ref, wa_ref, wb_ref, acc_ref, q_ref, g_ref, after_ref, total_ref, run):
    depth = q_ref.shape[2]

    @pl.when(pl.program_id(0) == 0)
    def _():
        run[...] = jnp.zeros_like(run)

    total = acc_ref[...] + dot(a_ref[...], wa_ref[...], 1, 1)
    total = (total + dot(b_ref[...], wb_ref[...], 1, 1)).astype(BF16)
    g_ref[...] = total
    for j in reversed(range(a_ref.shape[0] // BLOCK)):
        part = slice(j * BLOCK, (j + 1) * BLOCK)
        after_ref[j] = run[...]
        for h in range(heads):
            run[h] += dot(q_ref[h, part, :], total[part, h * depth : (h + 1) * depth], 0, 0)
    total_ref[...] = run[...].astype(BF16)


def attn_last(a, b, index, w, acc, q):
    tokens, width = a.shape
    rows = w.shape[0]
    heads, _, depth = q.shape
    steps = tokens // STEP
    last = steps - 1
    blocks = STEP // BLOCK
    piece = pl.BlockSpec((STEP, width), lambda s, i: (last - s, 0))
    wide = pl.BlockSpec((STEP, rows), lambda s, i: (last - s, 0))
    return pl.pallas_call(
        lambda *refs: attn_last_kernel(heads, *refs),
        grid_spec=pltpu.PrefetchScalarGridSpec(
            num_scalar_prefetch=1,
            grid=(steps,),
            in_specs=[
                piece,
                piece,
                pl.BlockSpec((rows, width), lambda s, i: (0, i[0])),
                pl.BlockSpec((rows, width), lambda s, i: (0, i[1])),
                wide,
                pl.BlockSpec((heads, STEP, depth), lambda s, i: (0, last - s, 0)),
            ],
            out_specs=[
                wide,
                pl.BlockSpec((blocks, heads, depth, depth), lambda s, i: (last - s, 0, 0, 0)),
                pl.BlockSpec((heads, depth, depth), lambda s, i: (0, 0, 0)),
            ],
            scratch_shapes=[pltpu.VMEM((heads, depth, depth), F32)],
        ),
        out_shape=[
            pltpu.HBM((tokens, rows), BF16),
            pltpu.HBM((tokens // BLOCK, heads, depth, depth), F32),
            jax.ShapeDtypeStruct((heads, depth, depth), BF16),
        ],
        compiler_params=params(18),
        cost_estimate=cost(5 * tokens * rows * width, 4 * tokens * rows),
        name="attn_last",
    )(index, a, b, w, w, acc, q)


def inner_kernel(heads, q_ref, k_ref, v_ref, g_ref, qi_ref, ki_ref, vi_ref):
    depth = q_ref.shape[2]
    row = lax.broadcasted_iota(jnp.int32, (BLOCK, BLOCK), 0)
    col = lax.broadcasted_iota(jnp.int32, (BLOCK, BLOCK), 1)
    for h in range(heads):
        lanes = slice(h * depth, (h + 1) * depth)
        q, k, v, g = q_ref[h], k_ref[h], v_ref[h], g_ref[:, lanes]
        grad = jnp.where(col <= row, dot(g, v, 1, 1), 0.0).astype(BF16)
        grad_t = jnp.where(row <= col, dot(v, g, 1, 1), 0.0).astype(BF16)
        score_t = jnp.where(row <= col, dot(k, q, 1, 1), 0.0).astype(BF16)
        qi_ref[:, lanes] = dot(grad, k, 1, 0)
        ki_ref[:, lanes] = dot(grad_t, q, 1, 0)
        vi_ref[:, lanes] = dot(score_t, g, 1, 0)


def inner(q, k, v, g):
    heads, tokens, depth = q.shape
    rows = heads * depth
    split = pl.BlockSpec((heads, BLOCK, depth), lambda b: (0, b, 0))
    wide = pl.BlockSpec((BLOCK, rows), lambda b: (b, 0))
    return pl.pallas_call(
        lambda *refs: inner_kernel(heads, *refs),
        grid=(tokens // BLOCK,),
        in_specs=[split, split, split, wide],
        out_specs=[wide] * 3,
        out_shape=[jax.ShapeDtypeStruct((tokens, rows), F32)] + [pltpu.HBM((tokens, rows), F32)] * 2,
        compiler_params=params(10),
        name="inner",
    )(q, k, v, g)


def query_kernel(heads, factor, g_ref, qi_ref, local_ref, far_ref, out_ref):
    depth = far_ref.shape[1]
    for j in range(g_ref.shape[0] // BLOCK):
        rows = slice(j * BLOCK, (j + 1) * BLOCK)
        parts = []
        for h in range(heads):
            lanes = slice(h * depth, (h + 1) * depth)
            state = (far_ref[h].astype(F32) + local_ref[j, h]).astype(BF16)
            parts.append(factor * (qi_ref[rows, lanes] + dot(g_ref[rows, lanes], state, 1, 1)))
        out_ref[rows] = jnp.concatenate(parts, 1).astype(BF16).reshape(BLOCK, heads, depth)


def query_out(g, qi, local, far, factor):
    tokens, rows = g.shape
    heads, depth, _ = far.shape
    step = STEP
    wide = pl.BlockSpec((step, rows), lambda b: (b, 0))
    return pl.pallas_call(
        lambda *refs: query_kernel(heads, factor, *refs),
        grid=(tokens // step,),
        in_specs=[
            wide,
            wide,
            pl.BlockSpec((step // BLOCK, heads, depth, depth), lambda b: (b, 0, 0, 0)),
            pl.BlockSpec((heads, depth, depth), lambda b: (0, 0, 0)),
        ],
        out_specs=pl.BlockSpec((step, heads, depth), lambda b: (b, 0, 0)),
        out_shape=jax.ShapeDtypeStruct((tokens, heads, depth), BF16),
        compiler_params=params(12),
        name="query_out",
    )(g, qi, local, far)


def key_value_kernel(heads, factor, k_ref, v_ref, ki_ref, vi_ref, local_ref, far_ref, ko_ref, vo_ref):
    depth = far_ref.shape[1]
    for j in range(ki_ref.shape[0] // BLOCK):
        rows = slice(j * BLOCK, (j + 1) * BLOCK)
        keys, values = [], []
        for h in range(heads):
            lanes = slice(h * depth, (h + 1) * depth)
            state = (far_ref[h].astype(F32) + local_ref[j, h]).astype(BF16)
            keys.append(factor * (ki_ref[rows, lanes] + dot(v_ref[h, rows, :], state, 1, 1)))
            values.append(factor * (vi_ref[rows, lanes] + dot(k_ref[h, rows, :], state, 1, 0)))
        ko_ref[rows] = jnp.concatenate(keys, 1).astype(BF16).reshape(BLOCK, heads, depth)
        vo_ref[rows] = jnp.concatenate(values, 1).astype(BF16).reshape(BLOCK, heads, depth)


def key_value_out(k, v, ki, vi, local, far, factor):
    tokens, rows = ki.shape
    heads, depth, _ = far.shape
    split = pl.BlockSpec((heads, STEP, depth), lambda b: (0, b, 0))
    step = STEP
    wide = pl.BlockSpec((step, rows), lambda b: (b, 0))
    out = pl.BlockSpec((step, heads, depth), lambda b: (b, 0, 0))
    return pl.pallas_call(
        lambda *refs: key_value_kernel(heads, factor, *refs),
        grid=(tokens // step,),
        in_specs=[
            split,
            split,
            wide,
            wide,
            pl.BlockSpec((step // BLOCK, heads, depth, depth), lambda b: (b, 0, 0, 0)),
            pl.BlockSpec((heads, depth, depth), lambda b: (0, 0, 0)),
        ],
        out_specs=[out, out],
        out_shape=[jax.ShapeDtypeStruct((tokens, heads, depth), BF16)] * 2,
        compiler_params=params(18),
        name="key_value_out",
    )(k, v, ki, vi, local, far)


def body(queries, key_rows, value_rows, out_grad, out_weight):
    tokens, heads, depth = queries.shape
    shards = lax.axis_size("seq")
    columns = lax.axis_size("head")
    chips = columns // 2
    factor = 1.0 / math.sqrt(depth * tokens * shards)

    def along(shift):
        return [(2 * x + c, 2 * ((x + shift) % chips) + c) for x in range(chips) for c in range(2)]

    def send(array, pairs):
        return lax.ppermute(array, "head", pairs)

    swap = [(i, i ^ 1) for i in range(columns)]
    right, left = along(1), along(-1)
    half = tokens // 2

    me = lax.axis_index("head")
    chip, core = me // 2, me % 2

    def column(shift, other):
        return 2 * ((chip + shift) % chips) + (1 - core if other else core)

    w = out_weight.reshape(heads * depth, -1)

    def columns_of(*shifts):
        return jnp.stack([column(s, other) for s in shifts for other in (False, True)]).astype(jnp.int32)

    own_columns, near_columns, far_columns, out_grad = lax.optimization_barrier(
        (columns_of(0), columns_of(-1, 1), columns_of(2), out_grad)
    )
    from_left = send(out_grad, right)
    from_right = send(out_grad, left)

    q = queries.transpose(1, 0, 2)
    k = key_rows.transpose(1, 0, 2)
    v = value_rows.transpose(1, 0, 2)

    kv_local, kv_total = kv_states(k, v)
    kv_total, q, k, v = lax.optimization_barrier((kv_total, q, k, v))
    rows = heads * depth // shards
    kv_pieces = lax.all_to_all(kv_total.reshape(shards, rows, depth), "seq", 0, 0, tiled=True)
    earlier = jnp.tril(jnp.ones((shards, shards), BF16), -1)
    later = jnp.triu(jnp.ones((shards, shards), BF16), 1)

    def scan(mask, pieces):
        sums = dot(mask, pieces.reshape(shards, rows * depth), 1, 0)
        return sums.astype(BF16).reshape(shards, rows, depth)

    kv_sums = scan(earlier, kv_pieces)
    from_left, from_right, out_grad, kv_sums, q, k, v = lax.optimization_barrier(
        (from_left, from_right, out_grad, kv_sums, q, k, v)
    )
    far_top = send(from_left[:half], right)
    far_bottom = send(from_right[half:], left)
    from_left_twin = send(from_left, swap)
    from_right_twin = send(from_right, swap)
    twin = send(out_grad, swap)
    acc = attn_add(None, [out_grad, twin], own_columns, w, "attn_own")
    acc = attn_add(
        acc,
        [from_left, from_left_twin, from_right, from_right_twin],
        near_columns,
        w,
        "attn_near",
    )
    far_top, far_bottom, acc = lax.optimization_barrier((far_top, far_bottom, acc))
    far_top_twin = send(far_top, swap)
    far_bottom_twin = send(far_bottom, swap)
    far = jnp.concatenate([far_top, far_bottom], 0)
    far_twin = jnp.concatenate([far_top_twin, far_bottom_twin], 0)
    grad, qg_local, qg_total = attn_last(far, far_twin, far_columns, w, acc, q)

    both = jnp.concatenate([qg_total.reshape(shards, rows, depth), kv_sums], 1)
    both = lax.all_to_all(both, "seq", 0, 0, tiled=True)
    qg_sums = scan(later, both[:, :rows])
    before = both[:, rows:].reshape(heads, depth, depth)
    after = lax.all_to_all(qg_sums, "seq", 0, 0, tiled=True).reshape(heads, depth, depth)

    qi, ki, vi = inner(q, k, v, grad)
    ki, vi, qg_local = in_hbm(ki), in_hbm(vi), in_hbm(qg_local)
    query_grad = query_out(grad, qi, kv_local, before, factor)
    key_grad, value_grad = key_value_out(k, v, ki, vi, qg_local, after, factor)
    return query_grad, key_grad, value_grad


def solution(mesh):
    placed = (
        P("seq", "head", None),
        P("seq", "head", None),
        P("seq", "head", None),
        P("seq", "head"),
        P("head", None, None),
    )
    return jax.shard_map(
        body,
        mesh=mesh,
        in_specs=placed,
        out_specs=(P("seq", "head", None), P("seq", "head", None), P("seq", "head", None)),
        check_vma=False,
    )
```

```python
import math

import jax
import jax.numpy as jnp
from jax import lax
from jax.experimental import pallas as pl
from jax.experimental.pallas import tpu as pltpu
from jax.sharding import PartitionSpec as P

BLOCK = 256
STEP = 512
F32 = jnp.float32
BF16 = jnp.bfloat16


def dot(a, b, ca, cb):
    return lax.dot_general(a, b, (((ca,), (cb,)), ((), ())), preferred_element_type=F32)


def params(mib):
    return pltpu.CompilerParams(vmem_limit_bytes=mib * 1024 * 1024)


def in_hbm(array):
    return pltpu.with_memory_space_constraint(array, pltpu.HBM)


def cost(flops, moved):
    return pl.CostEstimate(flops=flops, bytes_accessed=moved, transcendentals=0)


def kv_kernel(heads, k_ref, v_ref, before_ref, total_ref, run):
    step = pl.program_id(0)

    @pl.when(step == 0)
    def _():
        run[...] = jnp.zeros_like(run)

    before_ref[0] = run[...]
    for h in range(heads):
        run[h] += dot(k_ref[h], v_ref[h], 0, 0)
    total_ref[...] = run[...].astype(BF16)


def kv_states(k, v):
    heads, tokens, depth = k.shape
    blocks = tokens // BLOCK
    spec = pl.BlockSpec((heads, BLOCK, depth), lambda b: (0, b, 0))
    return pl.pallas_call(
        lambda *refs: kv_kernel(heads, *refs),
        grid=(blocks,),
        in_specs=[spec, spec],
        out_specs=[
            pl.BlockSpec((1, heads, depth, depth), lambda b: (b, 0, 0, 0)),
            pl.BlockSpec((heads, depth, depth), lambda b: (0, 0, 0)),
        ],
        out_shape=[
            pltpu.HBM((blocks, heads, depth, depth), F32),
            jax.ShapeDtypeStruct((heads, depth, depth), BF16),
        ],
        scratch_shapes=[pltpu.VMEM((heads, depth, depth), F32)],
        compiler_params=params(6),
        name="kv_states",
    )(k, v)


def attn_add_kernel(count, acc_ref, *refs):
    total = None if acc_ref is None else acc_ref[...]
    for i in range(count):
        part = dot(refs[i][...], refs[count + i][...], 1, 1)
        total = part if total is None else total + part
    refs[-1][...] = total


def attn_add(acc, pieces, index, w, name):
    tokens, width = pieces[0].shape
    rows = w.shape[0]
    count = len(pieces)
    spec = pl.BlockSpec((BLOCK, width), lambda b, i: (b, 0))
    wide = pl.BlockSpec((BLOCK, rows), lambda b, i: (b, 0))
    weights = [pl.BlockSpec((rows, width), lambda b, i, j=j: (0, i[j])) for j in range(count)]
    first = [] if acc is None else [acc]
    return pl.pallas_call(
        lambda i, *refs: attn_add_kernel(count, *(refs if first else (None, *refs))),
        grid_spec=pltpu.PrefetchScalarGridSpec(
            num_scalar_prefetch=1,
            grid=(tokens // BLOCK,),
            in_specs=[wide] * len(first) + [spec] * count + weights,
            out_specs=wide,
        ),
        out_shape=jax.ShapeDtypeStruct((tokens, rows), F32),
        compiler_params=params(6 + 3 * count),
        cost_estimate=cost(2 * tokens * rows * width * count, 4 * tokens * rows),
        name=name,
    )(index, *first, *pieces, *([w] * count))


def attn_last_kernel(heads, i_ref, a_ref, wa_ref, acc_ref, q_ref, g_ref, after_ref, total_ref, run):
    depth = q_ref.shape[2]

    @pl.when(pl.program_id(0) == 0)
    def _():
        run[...] = jnp.zeros_like(run)

    total = (acc_ref[...] + dot(a_ref[...], wa_ref[...], 1, 1)).astype(BF16)
    g_ref[...] = total
    for j in reversed(range(a_ref.shape[0] // BLOCK)):
        part = slice(j * BLOCK, (j + 1) * BLOCK)
        after_ref[j] = run[...].astype(BF16)
        for h in range(heads):
            run[h] += dot(q_ref[h, part, :], total[part, h * depth : (h + 1) * depth], 0, 0)
    total_ref[...] = run[...].astype(BF16)


def attn_last(a, index, w, acc, q):
    tokens, width = a.shape
    rows = w.shape[0]
    heads, _, depth = q.shape
    steps = tokens // STEP
    last = steps - 1
    blocks = STEP // BLOCK
    piece = pl.BlockSpec((STEP, width), lambda s, i: (last - s, 0))
    wide = pl.BlockSpec((STEP, rows), lambda s, i: (last - s, 0))
    return pl.pallas_call(
        lambda *refs: attn_last_kernel(heads, *refs),
        grid_spec=pltpu.PrefetchScalarGridSpec(
            num_scalar_prefetch=1,
            grid=(steps,),
            in_specs=[
                piece,
                pl.BlockSpec((rows, width), lambda s, i: (0, i[0])),
                wide,
                pl.BlockSpec((heads, STEP, depth), lambda s, i: (0, last - s, 0)),
            ],
            out_specs=[
                wide,
                pl.BlockSpec((blocks, heads, depth, depth), lambda s, i: (last - s, 0, 0, 0)),
                pl.BlockSpec((heads, depth, depth), lambda s, i: (0, 0, 0)),
            ],
            scratch_shapes=[pltpu.VMEM((heads, depth, depth), F32)],
        ),
        out_shape=[
            pltpu.HBM((tokens, rows), BF16),
            pltpu.HBM((tokens // BLOCK, heads, depth, depth), BF16),
            jax.ShapeDtypeStruct((heads, depth, depth), BF16),
        ],
        compiler_params=params(18),
        cost_estimate=cost(5 * tokens * rows * width, 4 * tokens * rows),
        name="attn_last",
    )(index, a, w, acc, q)


def inner_kernel(heads, q_ref, k_ref, v_ref, g_ref, local_ref, qi_ref, ki_ref, vi_ref):
    depth = q_ref.shape[2]
    row = lax.broadcasted_iota(jnp.int32, (BLOCK, BLOCK), 0)
    col = lax.broadcasted_iota(jnp.int32, (BLOCK, BLOCK), 1)
    for h in range(heads):
        lanes = slice(h * depth, (h + 1) * depth)
        q, k, v, g = q_ref[h], k_ref[h], v_ref[h], g_ref[:, lanes]
        grad = jnp.where(col <= row, dot(g, v, 1, 1), 0.0).astype(BF16)
        grad_t = jnp.where(row <= col, dot(v, g, 1, 1), 0.0).astype(BF16)
        score_t = jnp.where(row <= col, dot(k, q, 1, 1), 0.0).astype(BF16)
        qi_ref[:, lanes] = dot(grad, k, 1, 0)
        local = local_ref[0, h]
        ki_ref[:, lanes] = (dot(grad_t, q, 1, 0) + dot(v, local, 1, 1)).astype(BF16)
        vi_ref[:, lanes] = (dot(score_t, g, 1, 0) + dot(k, local, 1, 0)).astype(BF16)


def inner(q, k, v, g, local):
    heads, tokens, depth = q.shape
    rows = heads * depth
    split = pl.BlockSpec((heads, BLOCK, depth), lambda b: (0, b, 0))
    wide = pl.BlockSpec((BLOCK, rows), lambda b: (b, 0))
    return pl.pallas_call(
        lambda *refs: inner_kernel(heads, *refs),
        grid=(tokens // BLOCK,),
        in_specs=[
            split,
            split,
            split,
            wide,
            pl.BlockSpec((1, heads, depth, depth), lambda b: (b, 0, 0, 0)),
        ],
        out_specs=[wide] * 3,
        out_shape=[jax.ShapeDtypeStruct((tokens, rows), F32)] + [pltpu.HBM((tokens, rows), BF16)] * 2,
        compiler_params=params(10),
        name="inner",
    )(q, k, v, g, local)


def query_kernel(heads, factor, g_ref, qi_ref, local_ref, far_ref, out_ref):
    depth = far_ref.shape[1]
    for j in range(g_ref.shape[0] // BLOCK):
        rows = slice(j * BLOCK, (j + 1) * BLOCK)
        parts = []
        for h in range(heads):
            lanes = slice(h * depth, (h + 1) * depth)
            state = (far_ref[h].astype(F32) + local_ref[j, h]).astype(BF16)
            parts.append(factor * (qi_ref[rows, lanes] + dot(g_ref[rows, lanes], state, 1, 1)))
        out_ref[rows] = jnp.concatenate(parts, 1).astype(BF16).reshape(BLOCK, heads, depth)


def query_out(g, qi, local, far, factor):
    tokens, rows = g.shape
    heads, depth, _ = far.shape
    step = STEP
    wide = pl.BlockSpec((step, rows), lambda b: (b, 0))
    return pl.pallas_call(
        lambda *refs: query_kernel(heads, factor, *refs),
        grid=(tokens // step,),
        in_specs=[
            wide,
            wide,
            pl.BlockSpec((step // BLOCK, heads, depth, depth), lambda b: (b, 0, 0, 0)),
            pl.BlockSpec((heads, depth, depth), lambda b: (0, 0, 0)),
        ],
        out_specs=pl.BlockSpec((step, heads, depth), lambda b: (b, 0, 0)),
        out_shape=jax.ShapeDtypeStruct((tokens, heads, depth), BF16),
        compiler_params=params(12),
        name="query_out",
    )(g, qi, local, far)


def key_value_kernel(heads, factor, k_ref, v_ref, ki_ref, vi_ref, far_ref, ko_ref, vo_ref):
    depth = far_ref.shape[1]
    keys, values = [], []
    for h in range(heads):
        lanes = slice(h * depth, (h + 1) * depth)
        state = far_ref[h]
        keys.append(factor * (ki_ref[:, lanes].astype(F32) + dot(v_ref[h], state, 1, 1)))
        values.append(factor * (vi_ref[:, lanes].astype(F32) + dot(k_ref[h], state, 1, 0)))
    ko_ref[...] = jnp.concatenate(keys, 1).astype(BF16).reshape(ko_ref.shape)
    vo_ref[...] = jnp.concatenate(values, 1).astype(BF16).reshape(vo_ref.shape)


def key_value_out(k, v, ki, vi, far, factor, step=STEP):
    tokens, rows = ki.shape
    heads, depth, _ = far.shape
    split = pl.BlockSpec((heads, step, depth), lambda b: (0, b, 0))
    wide = pl.BlockSpec((step, rows), lambda b: (b, 0))
    out = pl.BlockSpec((step, heads, depth), lambda b: (b, 0, 0))
    return pl.pallas_call(
        lambda *refs: key_value_kernel(heads, factor, *refs),
        grid=(tokens // step,),
        in_specs=[
            split,
            split,
            wide,
            wide,
            pl.BlockSpec((heads, depth, depth), lambda b: (0, 0, 0)),
        ],
        out_specs=[out, out],
        out_shape=[jax.ShapeDtypeStruct((tokens, heads, depth), BF16)] * 2,
        compiler_params=params(18),
        name="key_value_out",
    )(k, v, ki, vi, far)


def body(queries, key_rows, value_rows, out_grad, out_weight):
    tokens, heads, depth = queries.shape
    shards = lax.axis_size("seq")
    columns = lax.axis_size("head")
    chips = columns // 2
    factor = 1.0 / math.sqrt(depth * tokens * shards)

    def along(shift):
        return [(2 * x + c, 2 * ((x + shift) % chips) + c) for x in range(chips) for c in range(2)]

    def send(array, pairs):
        return lax.ppermute(array, "head", pairs)

    swap = [(i, i ^ 1) for i in range(columns)]
    right, left = along(1), along(-1)
    half = tokens // 2

    me = lax.axis_index("head")
    chip, core = me // 2, me % 2

    def column(shift, other):
        return 2 * ((chip + shift) % chips) + (1 - core if other else core)

    w = out_weight.reshape(heads * depth, -1)

    def columns_of(*shifts):
        return jnp.stack([column(s, other) for s in shifts for other in (False, True)]).astype(jnp.int32)

    near_columns, far_columns, out_grad = lax.optimization_barrier(
        (columns_of(0, -1, 1), (columns_of(2)[:1], columns_of(2)[1:]), out_grad)
    )
    from_left = send(out_grad, right)
    from_right = send(out_grad, left)
    twin = send(out_grad, swap)

    k = key_rows.transpose(1, 0, 2)
    v = value_rows.transpose(1, 0, 2)

    kv_local, kv_total = kv_states(k, v)
    order = jnp.arange(shards)
    later = (order[:, None] < order[None, :]).astype(BF16)
    earlier = (order[:, None] > order[None, :]).astype(BF16)
    kv_total, k, v, later, earlier, queries, twin = lax.optimization_barrier(
        (kv_total, k, v, later, earlier, queries, twin)
    )
    rows = heads * depth // shards
    kv_pieces = lax.all_to_all(kv_total.reshape(shards, rows, depth), "seq", 0, 0, tiled=True)

    def scan(mask, pieces):
        sums = dot(mask, pieces.reshape(shards, rows * depth), 1, 0)
        return sums.astype(BF16).reshape(shards, rows, depth)

    kv_sums = scan(earlier, kv_pieces)
    from_left, from_right, kv_sums, queries, k, v = lax.optimization_barrier(
        (from_left, from_right, kv_sums, queries, k, v)
    )
    q = queries.transpose(1, 0, 2)
    to_right, to_left, near_left, near_right = lax.optimization_barrier(
        (from_left[:half], from_right[half:], from_left, from_right)
    )
    far_top = send(to_right, right)
    far_bottom = send(to_left, left)
    from_left_twin = send(near_left, swap)
    from_right_twin = send(near_right, swap)
    acc = attn_add(
        None,
        [out_grad, twin, from_left, from_left_twin, from_right, from_right_twin],
        near_columns,
        w,
        "attn_near",
    )
    far_top, far_bottom, acc, q = lax.optimization_barrier((far_top, far_bottom, acc, q))
    far = jnp.concatenate([far_top, far_bottom], 0)
    far_twin = send(far, swap)
    acc = attn_add(acc, [far], far_columns[0], w, "attn_far")
    far_twin, acc = lax.optimization_barrier((far_twin, acc))
    grad, qg_local, qg_total = attn_last(far_twin, far_columns[1], w, acc, q)

    both = jnp.concatenate([qg_total.reshape(shards, rows, depth), kv_sums], 1)
    both = lax.all_to_all(both, "seq", 0, 0, tiled=True)
    qg_sums = scan(later, both[:, :rows])
    before = both[:, rows:].reshape(heads, depth, depth)
    after = lax.all_to_all(qg_sums, "seq", 0, 0, tiled=True).reshape(heads, depth, depth)

    qi, ki, vi = inner(q, k, v, grad, qg_local)
    ki, vi = in_hbm(ki), in_hbm(vi)
    query_grad = query_out(grad, qi, kv_local, before, factor)
    key_grad, value_grad = key_value_out(k, v, ki, vi, after, factor)
    return query_grad, key_grad, value_grad


def solution(mesh):
    placed = (
        P("seq", "head", None),
        P("seq", "head", None),
        P("seq", "head", None),
        P("seq", "head"),
        P("head", None, None),
    )
    return jax.shard_map(
        body,
        mesh=mesh,
        in_specs=placed,
        out_specs=(P("seq", "head", None), P("seq", "head", None), P("seq", "head", None)),
        check_vma=False,
    )
```

```python
import math

import jax
import jax.numpy as jnp
from jax import lax
from jax.experimental import pallas as pl
from jax.experimental.pallas import tpu as pltpu
from jax.sharding import PartitionSpec as P

BLOCK = 256
STEP = 512
F32 = jnp.float32
BF16 = jnp.bfloat16


def dot(a, b, ca, cb):
    return lax.dot_general(a, b, (((ca,), (cb,)), ((), ())), preferred_element_type=F32)


def params(mib):
    return pltpu.CompilerParams(vmem_limit_bytes=mib * 1024 * 1024)


def in_hbm(array):
    return pltpu.with_memory_space_constraint(array, pltpu.HBM)


def cost(flops, moved):
    return pl.CostEstimate(flops=flops, bytes_accessed=moved, transcendentals=0)


def kv_kernel(heads, k_ref, v_ref, before_ref, total_ref, run):
    step = pl.program_id(0)

    @pl.when(step == 0)
    def _():
        run[...] = jnp.zeros_like(run)

    before_ref[0] = run[...]
    for h in range(heads):
        run[h] += dot(k_ref[h], v_ref[h], 0, 0)
    total_ref[...] = run[...].astype(BF16)


def kv_states(k, v):
    heads, tokens, depth = k.shape
    blocks = tokens // BLOCK
    spec = pl.BlockSpec((heads, BLOCK, depth), lambda b: (0, b, 0))
    return pl.pallas_call(
        lambda *refs: kv_kernel(heads, *refs),
        grid=(blocks,),
        in_specs=[spec, spec],
        out_specs=[
            pl.BlockSpec((1, heads, depth, depth), lambda b: (b, 0, 0, 0)),
            pl.BlockSpec((heads, depth, depth), lambda b: (0, 0, 0)),
        ],
        out_shape=[
            pltpu.HBM((blocks, heads, depth, depth), F32),
            jax.ShapeDtypeStruct((heads, depth, depth), BF16),
        ],
        scratch_shapes=[pltpu.VMEM((heads, depth, depth), F32)],
        compiler_params=params(6),
        name="kv_states",
    )(k, v)


def column_at(shift, other):
    me = lax.axis_index("head")
    count = lax.axis_size("head")
    twin = 1 - 2 * lax.rem(me, 2) if other else 0
    return lax.rem(me + twin + (2 * shift + count), count)


def attn_add_kernel(count, acc_ref, *refs):
    total = None if acc_ref is None else acc_ref[...]
    for i in range(count):
        part = dot(refs[i][...], refs[count + i][...], 1, 1)
        total = part if total is None else total + part
    refs[-1][...] = total


def attn_add(acc, pieces, places, w, name):
    tokens, width = pieces[0].shape
    rows = w.shape[0]
    count = len(pieces)
    spec = pl.BlockSpec((BLOCK, width), lambda b: (b, 0))
    wide = pl.BlockSpec((BLOCK, rows), lambda b: (b, 0))
    weights = [pl.BlockSpec((rows, width), lambda b, p=p: (0, column_at(*p))) for p in places]
    first = [] if acc is None else [acc]
    return pl.pallas_call(
        lambda *refs: attn_add_kernel(count, *(refs if first else (None, *refs))),
        grid=(tokens // BLOCK,),
        in_specs=[wide] * len(first) + [spec] * count + weights,
        out_specs=wide,
        out_shape=jax.ShapeDtypeStruct((tokens, rows), F32),
        compiler_params=params(6 + 3 * count),
        cost_estimate=cost(2 * tokens * rows * width * count, 4 * tokens * rows),
        name=name,
    )(*first, *pieces, *([w] * count))


def attn_last_kernel(heads, a_ref, wa_ref, acc_ref, q_ref, g_ref, after_ref, total_ref, run):
    depth = q_ref.shape[2]

    @pl.when(pl.program_id(0) == 0)
    def _():
        run[...] = jnp.zeros_like(run)

    total = (acc_ref[...] + dot(a_ref[...], wa_ref[...], 1, 1)).astype(BF16)
    g_ref[...] = total
    for j in reversed(range(a_ref.shape[0] // BLOCK)):
        part = slice(j * BLOCK, (j + 1) * BLOCK)
        after_ref[j] = run[...].astype(BF16)
        for h in range(heads):
            run[h] += dot(q_ref[h, part, :], total[part, h * depth : (h + 1) * depth], 0, 0)
    total_ref[...] = run[...].astype(BF16)


def attn_last(a, place, w, acc, q):
    tokens, width = a.shape
    rows = w.shape[0]
    heads, _, depth = q.shape
    steps = tokens // STEP
    last = steps - 1
    blocks = STEP // BLOCK
    piece = pl.BlockSpec((STEP, width), lambda s: (last - s, 0))
    wide = pl.BlockSpec((STEP, rows), lambda s: (last - s, 0))
    return pl.pallas_call(
        lambda *refs: attn_last_kernel(heads, *refs),
        grid=(steps,),
        in_specs=[
            piece,
            pl.BlockSpec((rows, width), lambda s: (0, column_at(*place))),
            wide,
            pl.BlockSpec((heads, STEP, depth), lambda s: (0, last - s, 0)),
        ],
        out_specs=[
            wide,
            pl.BlockSpec((blocks, heads, depth, depth), lambda s: (last - s, 0, 0, 0)),
            pl.BlockSpec((heads, depth, depth), lambda s: (0, 0, 0)),
        ],
        scratch_shapes=[pltpu.VMEM((heads, depth, depth), F32)],
        out_shape=[
            pltpu.HBM((tokens, rows), BF16),
            pltpu.HBM((tokens // BLOCK, heads, depth, depth), BF16),
            jax.ShapeDtypeStruct((heads, depth, depth), BF16),
        ],
        compiler_params=params(18),
        cost_estimate=cost(5 * tokens * rows * width, 4 * tokens * rows),
        name="attn_last",
    )(a, w, acc, q)


def inner_kernel(heads, q_ref, k_ref, v_ref, g_ref, local_ref, qi_ref, ki_ref, vi_ref):
    depth = q_ref.shape[2]
    row = lax.broadcasted_iota(jnp.int32, (BLOCK, BLOCK), 0)
    col = lax.broadcasted_iota(jnp.int32, (BLOCK, BLOCK), 1)
    for h in range(heads):
        lanes = slice(h * depth, (h + 1) * depth)
        q, k, v, g = q_ref[h], k_ref[h], v_ref[h], g_ref[:, lanes]
        grad = jnp.where(col <= row, dot(g, v, 1, 1), 0.0).astype(BF16)
        grad_t = jnp.where(row <= col, dot(v, g, 1, 1), 0.0).astype(BF16)
        score_t = jnp.where(row <= col, dot(k, q, 1, 1), 0.0).astype(BF16)
        qi_ref[:, lanes] = dot(grad, k, 1, 0)
        local = local_ref[0, h]
        ki_ref[:, lanes] = (dot(grad_t, q, 1, 0) + dot(v, local, 1, 1)).astype(BF16)
        vi_ref[:, lanes] = (dot(score_t, g, 1, 0) + dot(k, local, 1, 0)).astype(BF16)


def inner(q, k, v, g, local):
    heads, tokens, depth = q.shape
    rows = heads * depth
    split = pl.BlockSpec((heads, BLOCK, depth), lambda b: (0, b, 0))
    wide = pl.BlockSpec((BLOCK, rows), lambda b: (b, 0))
    return pl.pallas_call(
        lambda *refs: inner_kernel(heads, *refs),
        grid=(tokens // BLOCK,),
        in_specs=[
            split,
            split,
            split,
            wide,
            pl.BlockSpec((1, heads, depth, depth), lambda b: (b, 0, 0, 0)),
        ],
        out_specs=[wide] * 3,
        out_shape=[jax.ShapeDtypeStruct((tokens, rows), F32)] + [pltpu.HBM((tokens, rows), BF16)] * 2,
        compiler_params=params(10),
        name="inner",
    )(q, k, v, g, local)


def query_kernel(heads, factor, g_ref, qi_ref, local_ref, far_ref, out_ref):
    depth = far_ref.shape[1]
    for j in range(g_ref.shape[0] // BLOCK):
        rows = slice(j * BLOCK, (j + 1) * BLOCK)
        parts = []
        for h in range(heads):
            lanes = slice(h * depth, (h + 1) * depth)
            state = (far_ref[h].astype(F32) + local_ref[j, h]).astype(BF16)
            parts.append(factor * (qi_ref[rows, lanes] + dot(g_ref[rows, lanes], state, 1, 1)))
        out_ref[rows] = jnp.concatenate(parts, 1).astype(BF16).reshape(BLOCK, heads, depth)


def query_out(g, qi, local, far, factor):
    tokens, rows = g.shape
    heads, depth, _ = far.shape
    step = STEP
    wide = pl.BlockSpec((step, rows), lambda b: (b, 0))
    return pl.pallas_call(
        lambda *refs: query_kernel(heads, factor, *refs),
        grid=(tokens // step,),
        in_specs=[
            wide,
            wide,
            pl.BlockSpec((step // BLOCK, heads, depth, depth), lambda b: (b, 0, 0, 0)),
            pl.BlockSpec((heads, depth, depth), lambda b: (0, 0, 0)),
        ],
        out_specs=pl.BlockSpec((step, heads, depth), lambda b: (b, 0, 0)),
        out_shape=jax.ShapeDtypeStruct((tokens, heads, depth), BF16),
        compiler_params=params(12),
        name="query_out",
    )(g, qi, local, far)


def key_value_kernel(heads, factor, k_ref, v_ref, ki_ref, vi_ref, far_ref, ko_ref, vo_ref):
    depth = far_ref.shape[1]
    keys, values = [], []
    for h in range(heads):
        lanes = slice(h * depth, (h + 1) * depth)
        state = far_ref[h]
        keys.append(factor * (ki_ref[:, lanes].astype(F32) + dot(v_ref[h], state, 1, 1)))
        values.append(factor * (vi_ref[:, lanes].astype(F32) + dot(k_ref[h], state, 1, 0)))
    ko_ref[...] = jnp.concatenate(keys, 1).astype(BF16).reshape(ko_ref.shape)
    vo_ref[...] = jnp.concatenate(values, 1).astype(BF16).reshape(vo_ref.shape)


def key_value_out(k, v, ki, vi, far, factor, step=STEP):
    tokens, rows = ki.shape
    heads, depth, _ = far.shape
    split = pl.BlockSpec((heads, step, depth), lambda b: (0, b, 0))
    wide = pl.BlockSpec((step, rows), lambda b: (b, 0))
    out = pl.BlockSpec((step, heads, depth), lambda b: (b, 0, 0))
    return pl.pallas_call(
        lambda *refs: key_value_kernel(heads, factor, *refs),
        grid=(tokens // step,),
        in_specs=[
            split,
            split,
            wide,
            wide,
            pl.BlockSpec((heads, depth, depth), lambda b: (0, 0, 0)),
        ],
        out_specs=[out, out],
        out_shape=[jax.ShapeDtypeStruct((tokens, heads, depth), BF16)] * 2,
        compiler_params=params(18),
        name="key_value_out",
    )(k, v, ki, vi, far)


def body(queries, key_rows, value_rows, out_grad, out_weight):
    tokens, heads, depth = queries.shape
    shards = lax.axis_size("seq")
    columns = lax.axis_size("head")
    chips = columns // 2
    factor = 1.0 / math.sqrt(depth * tokens * shards)

    def along(shift):
        return [(2 * x + c, 2 * ((x + shift) % chips) + c) for x in range(chips) for c in range(2)]

    def send(array, pairs):
        return lax.ppermute(array, "head", pairs)

    swap = [(i, i ^ 1) for i in range(columns)]
    right, left = along(1), along(-1)
    half = tokens // 2

    w = out_weight.reshape(heads * depth, -1)

    from_left = send(out_grad, right)
    from_right = send(out_grad, left)

    k = key_rows.transpose(1, 0, 2)
    v = value_rows.transpose(1, 0, 2)

    kv_local, kv_total = kv_states(k, v)
    order = jnp.arange(shards)
    later = (order[:, None] < order[None, :]).astype(BF16)
    earlier = (order[:, None] > order[None, :]).astype(BF16)
    kv_total, k, v, later, earlier, queries = lax.optimization_barrier(
        (kv_total, k, v, later, earlier, queries)
    )
    rows = heads * depth // shards
    kv_pieces = lax.all_to_all(kv_total.reshape(shards, rows, depth), "seq", 0, 0, tiled=True)

    def scan(mask, pieces):
        sums = dot(mask, pieces.reshape(shards, rows * depth), 1, 0)
        return sums.astype(BF16).reshape(shards, rows, depth)

    kv_sums = scan(earlier, kv_pieces)
    from_left, from_right, kv_sums, queries, k, v, out_grad = lax.optimization_barrier(
        (from_left, from_right, kv_sums, queries, k, v, out_grad)
    )
    q = queries.transpose(1, 0, 2)
    to_right, to_left, near_left, near_right = lax.optimization_barrier(
        (from_left[:half], from_right[half:], from_left, from_right)
    )
    far_top = send(to_right, right)
    far_bottom = send(to_left, left)
    twin = send(out_grad, swap)
    from_left_twin = send(near_left, swap)
    from_right_twin = send(near_right, swap)
    acc = attn_add(
        None,
        [out_grad, twin, from_left, from_left_twin, from_right, from_right_twin],
        [(shift, other) for shift in (0, -1, 1) for other in (False, True)],
        w,
        "attn_near",
    )
    far_top, far_bottom, acc, q = lax.optimization_barrier((far_top, far_bottom, acc, q))
    far = jnp.concatenate([far_top, far_bottom], 0)
    far_twin = send(far, swap)
    acc = attn_add(acc, [far], [(2, False)], w, "attn_far")
    far_twin, acc = lax.optimization_barrier((far_twin, acc))
    grad, qg_local, qg_total = attn_last(far_twin, (2, True), w, acc, q)

    both = jnp.concatenate([qg_total.reshape(shards, rows, depth), kv_sums], 1)
    both = lax.all_to_all(both, "seq", 0, 0, tiled=True)
    qg_sums = scan(later, both[:, :rows])
    before = both[:, rows:].reshape(heads, depth, depth)
    after = lax.all_to_all(qg_sums, "seq", 0, 0, tiled=True).reshape(heads, depth, depth)

    qi, ki, vi = inner(q, k, v, grad, qg_local)
    ki, vi = in_hbm(ki), in_hbm(vi)
    query_grad = query_out(grad, qi, kv_local, before, factor)
    key_grad, value_grad = key_value_out(k, v, ki, vi, after, factor)
    return query_grad, key_grad, value_grad


def solution(mesh):
    placed = (
        P("seq", "head", None),
        P("seq", "head", None),
        P("seq", "head", None),
        P("seq", "head"),
        P("head", None, None),
    )
    return jax.shard_map(
        body,
        mesh=mesh,
        in_specs=placed,
        out_specs=(P("seq", "head", None), P("seq", "head", None), P("seq", "head", None)),
        check_vma=False,
    )
```

```python
import math

import jax
import jax.numpy as jnp
from jax import lax
from jax.experimental import pallas as pl
from jax.experimental.pallas import tpu as pltpu
from jax.sharding import PartitionSpec as P

BLOCK = 256
STEP = 512
F32 = jnp.float32
BF16 = jnp.bfloat16


def dot(a, b, ca, cb):
    return lax.dot_general(a, b, (((ca,), (cb,)), ((), ())), preferred_element_type=F32)


def params(mib):
    return pltpu.CompilerParams(vmem_limit_bytes=mib * 1024 * 1024)


def in_hbm(array):
    return pltpu.with_memory_space_constraint(array, pltpu.HBM)


def cost(flops, moved):
    return pl.CostEstimate(flops=flops, bytes_accessed=moved, transcendentals=0)


def kv_kernel(heads, k_ref, v_ref, before_ref, total_ref, run):
    step = pl.program_id(0)

    @pl.when(step == 0)
    def _():
        run[...] = jnp.zeros_like(run)

    before_ref[0] = run[...]
    for h in range(heads):
        run[h] += dot(k_ref[h], v_ref[h], 0, 0)
    total_ref[...] = run[...].astype(BF16)


def kv_states(k, v):
    heads, tokens, depth = k.shape
    blocks = tokens // BLOCK
    spec = pl.BlockSpec((heads, BLOCK, depth), lambda b: (0, b, 0))
    return pl.pallas_call(
        lambda *refs: kv_kernel(heads, *refs),
        grid=(blocks,),
        in_specs=[spec, spec],
        out_specs=[
            pl.BlockSpec((1, heads, depth, depth), lambda b: (b, 0, 0, 0)),
            pl.BlockSpec((heads, depth, depth), lambda b: (0, 0, 0)),
        ],
        out_shape=[
            pltpu.HBM((blocks, heads, depth, depth), F32),
            jax.ShapeDtypeStruct((heads, depth, depth), BF16),
        ],
        scratch_shapes=[pltpu.VMEM((heads, depth, depth), F32)],
        compiler_params=params(6),
        name="kv_states",
    )(k, v)


def column_at(shift, other):
    me = lax.axis_index("head")
    count = lax.axis_size("head")
    twin = 1 - 2 * lax.rem(me, 2) if other else 0
    return lax.rem(me + twin + (2 * shift + count), count)


def attn_add_kernel(count, acc_ref, *refs):
    total = None if acc_ref is None else acc_ref[...]
    for i in range(count):
        part = dot(refs[i][...], refs[count + i][...], 1, 1)
        total = part if total is None else total + part
    refs[-1][...] = total


def attn_add(acc, pieces, places, w, name):
    tokens, width = pieces[0].shape
    rows = w.shape[0]
    count = len(pieces)
    spec = pl.BlockSpec((BLOCK, width), lambda b: (b, 0))
    wide = pl.BlockSpec((BLOCK, rows), lambda b: (b, 0))
    weights = [pl.BlockSpec((rows, width), lambda b, p=p: (0, column_at(*p))) for p in places]
    first = [] if acc is None else [acc]
    return pl.pallas_call(
        lambda *refs: attn_add_kernel(count, *(refs if first else (None, *refs))),
        grid=(tokens // BLOCK,),
        in_specs=[wide] * len(first) + [spec] * count + weights,
        out_specs=wide,
        out_shape=jax.ShapeDtypeStruct((tokens, rows), F32),
        compiler_params=params(6 + 3 * count),
        cost_estimate=cost(2 * tokens * rows * width * count, 4 * tokens * rows),
        name=name,
    )(*first, *pieces, *([w] * count))


def attn_last_kernel(heads, a_ref, wa_ref, acc_ref, q_ref, g_ref, after_ref, total_ref, run):
    depth = q_ref.shape[2]

    @pl.when(pl.program_id(0) == 0)
    def _():
        run[...] = jnp.zeros_like(run)

    total = (acc_ref[...] + dot(a_ref[...], wa_ref[...], 1, 1)).astype(BF16)
    g_ref[...] = total
    for j in reversed(range(a_ref.shape[0] // BLOCK)):
        part = slice(j * BLOCK, (j + 1) * BLOCK)
        after_ref[j] = run[...].astype(BF16)
        for h in range(heads):
            run[h] += dot(q_ref[h, part, :], total[part, h * depth : (h + 1) * depth], 0, 0)
    total_ref[...] = run[...].astype(BF16)


def attn_last(a, place, w, acc, q):
    tokens, width = a.shape
    rows = w.shape[0]
    heads, _, depth = q.shape
    steps = tokens // STEP
    last = steps - 1
    blocks = STEP // BLOCK
    piece = pl.BlockSpec((STEP, width), lambda s: (last - s, 0))
    wide = pl.BlockSpec((STEP, rows), lambda s: (last - s, 0))
    return pl.pallas_call(
        lambda *refs: attn_last_kernel(heads, *refs),
        grid=(steps,),
        in_specs=[
            piece,
            pl.BlockSpec((rows, width), lambda s: (0, column_at(*place))),
            wide,
            pl.BlockSpec((heads, STEP, depth), lambda s: (0, last - s, 0)),
        ],
        out_specs=[
            wide,
            pl.BlockSpec((blocks, heads, depth, depth), lambda s: (last - s, 0, 0, 0)),
            pl.BlockSpec((heads, depth, depth), lambda s: (0, 0, 0)),
        ],
        scratch_shapes=[pltpu.VMEM((heads, depth, depth), F32)],
        out_shape=[
            pltpu.HBM((tokens, rows), BF16),
            pltpu.HBM((tokens // BLOCK, heads, depth, depth), BF16),
            jax.ShapeDtypeStruct((heads, depth, depth), BF16),
        ],
        compiler_params=params(18),
        cost_estimate=cost(5 * tokens * rows * width, 4 * tokens * rows),
        name="attn_last",
    )(a, w, acc, q)


def inner_kernel(heads, q_ref, k_ref, v_ref, g_ref, local_ref, qi_ref, ki_ref, vi_ref):
    depth = q_ref.shape[2]
    row = lax.broadcasted_iota(jnp.int32, (BLOCK, BLOCK), 0)
    col = lax.broadcasted_iota(jnp.int32, (BLOCK, BLOCK), 1)
    for h in range(heads):
        lanes = slice(h * depth, (h + 1) * depth)
        q, k, v, g = q_ref[h], k_ref[h], v_ref[h], g_ref[:, lanes]
        grad = jnp.where(col <= row, dot(g, v, 1, 1), 0.0).astype(BF16)
        grad_t = jnp.where(row <= col, dot(v, g, 1, 1), 0.0).astype(BF16)
        score_t = jnp.where(row <= col, dot(k, q, 1, 1), 0.0).astype(BF16)
        qi_ref[:, lanes] = dot(grad, k, 1, 0)
        local = local_ref[0, h]
        ki_ref[:, lanes] = (dot(grad_t, q, 1, 0) + dot(v, local, 1, 1)).astype(BF16)
        vi_ref[:, lanes] = (dot(score_t, g, 1, 0) + dot(k, local, 1, 0)).astype(BF16)


def inner(q, k, v, g, local):
    heads, tokens, depth = q.shape
    rows = heads * depth
    split = pl.BlockSpec((heads, BLOCK, depth), lambda b: (0, b, 0))
    wide = pl.BlockSpec((BLOCK, rows), lambda b: (b, 0))
    return pl.pallas_call(
        lambda *refs: inner_kernel(heads, *refs),
        grid=(tokens // BLOCK,),
        in_specs=[
            split,
            split,
            split,
            wide,
            pl.BlockSpec((1, heads, depth, depth), lambda b: (b, 0, 0, 0)),
        ],
        out_specs=[wide] * 3,
        out_shape=[jax.ShapeDtypeStruct((tokens, rows), F32)] + [pltpu.HBM((tokens, rows), BF16)] * 2,
        compiler_params=params(10),
        name="inner",
    )(q, k, v, g, local)


def query_kernel(heads, factor, g_ref, qi_ref, local_ref, far_ref, out_ref):
    depth = far_ref.shape[1]
    for j in range(g_ref.shape[0] // BLOCK):
        rows = slice(j * BLOCK, (j + 1) * BLOCK)
        parts = []
        for h in range(heads):
            lanes = slice(h * depth, (h + 1) * depth)
            state = (far_ref[h].astype(F32) + local_ref[j, h]).astype(BF16)
            parts.append(factor * (qi_ref[rows, lanes] + dot(g_ref[rows, lanes], state, 1, 1)))
        out_ref[rows] = jnp.concatenate(parts, 1).astype(BF16).reshape(BLOCK, heads, depth)


def query_out(g, qi, local, far, factor):
    tokens, rows = g.shape
    heads, depth, _ = far.shape
    step = STEP
    wide = pl.BlockSpec((step, rows), lambda b: (b, 0))
    return pl.pallas_call(
        lambda *refs: query_kernel(heads, factor, *refs),
        grid=(tokens // step,),
        in_specs=[
            wide,
            wide,
            pl.BlockSpec((step // BLOCK, heads, depth, depth), lambda b: (b, 0, 0, 0)),
            pl.BlockSpec((heads, depth, depth), lambda b: (0, 0, 0)),
        ],
        out_specs=pl.BlockSpec((step, heads, depth), lambda b: (b, 0, 0)),
        out_shape=jax.ShapeDtypeStruct((tokens, heads, depth), BF16),
        compiler_params=params(12),
        name="query_out",
    )(g, qi, local, far)


def key_value_kernel(heads, factor, k_ref, v_ref, ki_ref, vi_ref, far_ref, ko_ref, vo_ref):
    depth = far_ref.shape[1]
    keys, values = [], []
    for h in range(heads):
        lanes = slice(h * depth, (h + 1) * depth)
        state = far_ref[h]
        keys.append(factor * (ki_ref[:, lanes].astype(F32) + dot(v_ref[h], state, 1, 1)))
        values.append(factor * (vi_ref[:, lanes].astype(F32) + dot(k_ref[h], state, 1, 0)))
    ko_ref[...] = jnp.concatenate(keys, 1).astype(BF16).reshape(ko_ref.shape)
    vo_ref[...] = jnp.concatenate(values, 1).astype(BF16).reshape(vo_ref.shape)


def key_value_out(k, v, ki, vi, far, factor, step=STEP):
    tokens, rows = ki.shape
    heads, depth, _ = far.shape
    split = pl.BlockSpec((heads, step, depth), lambda b: (0, b, 0))
    wide = pl.BlockSpec((step, rows), lambda b: (b, 0))
    out = pl.BlockSpec((step, heads, depth), lambda b: (b, 0, 0))
    return pl.pallas_call(
        lambda *refs: key_value_kernel(heads, factor, *refs),
        grid=(tokens // step,),
        in_specs=[
            split,
            split,
            wide,
            wide,
            pl.BlockSpec((heads, depth, depth), lambda b: (0, 0, 0)),
        ],
        out_specs=[out, out],
        out_shape=[jax.ShapeDtypeStruct((tokens, heads, depth), BF16)] * 2,
        compiler_params=params(18),
        name="key_value_out",
    )(k, v, ki, vi, far)


def body(queries, key_rows, value_rows, out_grad, out_weight):
    tokens, heads, depth = queries.shape
    shards = lax.axis_size("seq")
    columns = lax.axis_size("head")
    chips = columns // 2
    factor = 1.0 / math.sqrt(depth * tokens * shards)

    def along(shift):
        return [(2 * x + c, 2 * ((x + shift) % chips) + c) for x in range(chips) for c in range(2)]

    def send(array, pairs):
        return lax.ppermute(array, "head", pairs)

    swap = [(i, i ^ 1) for i in range(columns)]
    right, left = along(1), along(-1)
    edge = 17 * tokens // 32

    w = out_weight.reshape(heads * depth, -1)

    from_left = send(out_grad, right)
    from_right = send(out_grad, left)

    k = key_rows.transpose(1, 0, 2)
    v = value_rows.transpose(1, 0, 2)

    kv_local, kv_total = kv_states(k, v)
    order = jnp.arange(shards)
    later = (order[:, None] < order[None, :]).astype(BF16)
    earlier = (order[:, None] > order[None, :]).astype(BF16)
    kv_total, k, v, later, earlier, queries = lax.optimization_barrier(
        (kv_total, k, v, later, earlier, queries)
    )
    rows = heads * depth // shards
    kv_pieces = lax.all_to_all(kv_total.reshape(shards, rows, depth), "seq", 0, 0, tiled=True)

    def scan(mask, pieces):
        sums = dot(mask, pieces.reshape(shards, rows * depth), 1, 0)
        return sums.astype(BF16).reshape(shards, rows, depth)

    kv_sums = scan(earlier, kv_pieces)
    from_left, from_right, kv_sums, queries, k, v, out_grad = lax.optimization_barrier(
        (from_left, from_right, kv_sums, queries, k, v, out_grad)
    )
    q = queries.transpose(1, 0, 2)
    to_right, to_left, near_left, near_right = lax.optimization_barrier(
        (from_left[:edge], from_right[edge:], from_left, from_right)
    )
    far_top = send(to_right, right)
    far_bottom = send(to_left, left)
    twin = send(out_grad, swap)
    from_left_twin = send(near_left, swap)
    from_right_twin = send(near_right, swap)
    acc = attn_add(
        None,
        [out_grad, twin, from_left, from_left_twin, from_right, from_right_twin],
        [(shift, other) for shift in (0, -1, 1) for other in (False, True)],
        w,
        "attn_near",
    )
    far_top, far_bottom, acc, q = lax.optimization_barrier((far_top, far_bottom, acc, q))
    far = jnp.concatenate([far_top, far_bottom], 0)
    far_twin = send(far, swap)
    acc = attn_add(acc, [far], [(2, False)], w, "attn_far")
    far_twin, acc = lax.optimization_barrier((far_twin, acc))
    grad, qg_local, qg_total = attn_last(far_twin, (2, True), w, acc, q)

    both = jnp.concatenate([qg_total.reshape(shards, rows, depth), kv_sums], 1)
    both = lax.all_to_all(both, "seq", 0, 0, tiled=True)
    qg_sums = scan(later, both[:, :rows])
    before = both[:, rows:].reshape(heads, depth, depth)
    after = lax.all_to_all(qg_sums, "seq", 0, 0, tiled=True).reshape(heads, depth, depth)

    qi, ki, vi = inner(q, k, v, grad, qg_local)
    ki, vi = in_hbm(ki), in_hbm(vi)
    query_grad = query_out(grad, qi, kv_local, before, factor)
    key_grad, value_grad = key_value_out(k, v, ki, vi, after, factor)
    return query_grad, key_grad, value_grad


def solution(mesh):
    placed = (
        P("seq", "head", None),
        P("seq", "head", None),
        P("seq", "head", None),
        P("seq", "head"),
        P("head", None, None),
    )
    return jax.shard_map(
        body,
        mesh=mesh,
        in_specs=placed,
        out_specs=(P("seq", "head", None), P("seq", "head", None), P("seq", "head", None)),
        check_vma=False,
    )
```

```python
import math

import jax
import jax.numpy as jnp
from jax import lax
from jax.experimental import pallas as pl
from jax.experimental.pallas import tpu as pltpu
from jax.sharding import PartitionSpec as P

BLOCK = 256
STEP = 512
F32 = jnp.float32
BF16 = jnp.bfloat16


def dot(a, b, ca, cb):
    return lax.dot_general(a, b, (((ca,), (cb,)), ((), ())), preferred_element_type=F32)


def params(mib):
    return pltpu.CompilerParams(vmem_limit_bytes=mib * 1024 * 1024)


def in_hbm(array):
    return pltpu.with_memory_space_constraint(array, pltpu.HBM)


def cost(flops, moved):
    return pl.CostEstimate(flops=flops, bytes_accessed=moved, transcendentals=0)


def kv_kernel(heads, k_ref, v_ref, before_ref, total_ref, run):
    step = pl.program_id(0)

    @pl.when(step == 0)
    def _():
        run[...] = jnp.zeros_like(run)

    before_ref[0] = run[...]
    for h in range(heads):
        run[h] += dot(k_ref[h], v_ref[h], 0, 0)
    total_ref[...] = run[...].astype(BF16)


def kv_states(k, v):
    heads, tokens, depth = k.shape
    blocks = tokens // BLOCK
    spec = pl.BlockSpec((heads, BLOCK, depth), lambda b: (0, b, 0))
    return pl.pallas_call(
        lambda *refs: kv_kernel(heads, *refs),
        grid=(blocks,),
        in_specs=[spec, spec],
        out_specs=[
            pl.BlockSpec((1, heads, depth, depth), lambda b: (b, 0, 0, 0)),
            pl.BlockSpec((heads, depth, depth), lambda b: (0, 0, 0)),
        ],
        out_shape=[
            pltpu.HBM((blocks, heads, depth, depth), F32),
            jax.ShapeDtypeStruct((heads, depth, depth), BF16),
        ],
        scratch_shapes=[pltpu.VMEM((heads, depth, depth), F32)],
        compiler_params=params(6),
        name="kv_states",
    )(k, v)


def column_at(shift, other):
    me = lax.axis_index("head")
    count = lax.axis_size("head")
    twin = 1 - 2 * lax.rem(me, 2) if other else 0
    return lax.rem(me + twin + (2 * shift + count), count)


def attn_add_kernel(count, acc_ref, *refs):
    total = None if acc_ref is None else acc_ref[...]
    for i in range(count):
        part = dot(refs[i][...], refs[count + i][...], 1, 1)
        total = part if total is None else total + part
    refs[-1][...] = total


def attn_add(acc, pieces, places, w, name):
    tokens, width = pieces[0].shape
    rows = w.shape[0]
    count = len(pieces)
    spec = pl.BlockSpec((BLOCK, width), lambda b: (b, 0))
    wide = pl.BlockSpec((BLOCK, rows), lambda b: (b, 0))
    weights = [pl.BlockSpec((rows, width), lambda b, p=p: (0, column_at(*p))) for p in places]
    first = [] if acc is None else [acc]
    return pl.pallas_call(
        lambda *refs: attn_add_kernel(count, *(refs if first else (None, *refs))),
        grid=(tokens // BLOCK,),
        in_specs=[wide] * len(first) + [spec] * count + weights,
        out_specs=wide,
        out_shape=jax.ShapeDtypeStruct((tokens, rows), F32),
        compiler_params=params(6 + 3 * count),
        cost_estimate=cost(2 * tokens * rows * width * count, 4 * tokens * rows),
        name=name,
    )(*first, *pieces, *([w] * count))


def attn_last_kernel(heads, a_ref, wa_ref, acc_ref, q_ref, g_ref, after_ref, total_ref, run):
    depth = q_ref.shape[2]

    @pl.when(pl.program_id(0) == 0)
    def _():
        run[...] = jnp.zeros_like(run)

    total = (acc_ref[...] + dot(a_ref[...], wa_ref[...], 1, 1)).astype(BF16)
    g_ref[...] = total
    for j in reversed(range(a_ref.shape[0] // BLOCK)):
        part = slice(j * BLOCK, (j + 1) * BLOCK)
        after_ref[j] = run[...].astype(BF16)
        for h in range(heads):
            run[h] += dot(q_ref[h, part, :], total[part, h * depth : (h + 1) * depth], 0, 0)
    total_ref[...] = run[...].astype(BF16)


def attn_last(a, place, w, acc, q):
    tokens, width = a.shape
    rows = w.shape[0]
    heads, _, depth = q.shape
    steps = tokens // BLOCK
    last = steps - 1
    blocks = 1
    piece = pl.BlockSpec((BLOCK, width), lambda s: (last - s, 0))
    wide = pl.BlockSpec((BLOCK, rows), lambda s: (last - s, 0))
    return pl.pallas_call(
        lambda *refs: attn_last_kernel(heads, *refs),
        grid=(steps,),
        in_specs=[
            piece,
            pl.BlockSpec((rows, width), lambda s: (0, column_at(*place))),
            wide,
            pl.BlockSpec((heads, BLOCK, depth), lambda s: (0, last - s, 0)),
        ],
        out_specs=[
            wide,
            pl.BlockSpec((blocks, heads, depth, depth), lambda s: (last - s, 0, 0, 0)),
            pl.BlockSpec((heads, depth, depth), lambda s: (0, 0, 0)),
        ],
        scratch_shapes=[pltpu.VMEM((heads, depth, depth), F32)],
        out_shape=[
            pltpu.HBM((tokens, rows), BF16),
            pltpu.HBM((tokens // BLOCK, heads, depth, depth), BF16),
            jax.ShapeDtypeStruct((heads, depth, depth), BF16),
        ],
        compiler_params=params(18),
        cost_estimate=cost(5 * tokens * rows * width, 4 * tokens * rows),
        name="attn_last",
    )(a, w, acc, q)


def inner_kernel(heads, q_ref, k_ref, v_ref, g_ref, local_ref, qi_ref, ki_ref, vi_ref):
    depth = q_ref.shape[2]
    row = lax.broadcasted_iota(jnp.int32, (BLOCK, BLOCK), 0)
    col = lax.broadcasted_iota(jnp.int32, (BLOCK, BLOCK), 1)
    for h in range(heads):
        lanes = slice(h * depth, (h + 1) * depth)
        q, k, v, g = q_ref[h], k_ref[h], v_ref[h], g_ref[:, lanes]
        grad = jnp.where(col <= row, dot(g, v, 1, 1), 0.0).astype(BF16)
        grad_t = jnp.where(row <= col, dot(v, g, 1, 1), 0.0).astype(BF16)
        score_t = jnp.where(row <= col, dot(k, q, 1, 1), 0.0).astype(BF16)
        qi_ref[:, lanes] = dot(grad, k, 1, 0)
        local = local_ref[0, h]
        ki_ref[:, lanes] = (dot(grad_t, q, 1, 0) + dot(v, local, 1, 1)).astype(BF16)
        vi_ref[:, lanes] = (dot(score_t, g, 1, 0) + dot(k, local, 1, 0)).astype(BF16)


def inner(q, k, v, g, local):
    heads, tokens, depth = q.shape
    rows = heads * depth
    split = pl.BlockSpec((heads, BLOCK, depth), lambda b: (0, b, 0))
    wide = pl.BlockSpec((BLOCK, rows), lambda b: (b, 0))
    return pl.pallas_call(
        lambda *refs: inner_kernel(heads, *refs),
        grid=(tokens // BLOCK,),
        in_specs=[
            split,
            split,
            split,
            wide,
            pl.BlockSpec((1, heads, depth, depth), lambda b: (b, 0, 0, 0)),
        ],
        out_specs=[wide] * 3,
        out_shape=[jax.ShapeDtypeStruct((tokens, rows), F32)] + [pltpu.HBM((tokens, rows), BF16)] * 2,
        compiler_params=params(10),
        name="inner",
    )(q, k, v, g, local)


def query_kernel(heads, factor, g_ref, qi_ref, local_ref, far_ref, out_ref):
    depth = far_ref.shape[1]
    for j in range(g_ref.shape[0] // BLOCK):
        rows = slice(j * BLOCK, (j + 1) * BLOCK)
        parts = []
        for h in range(heads):
            lanes = slice(h * depth, (h + 1) * depth)
            state = (far_ref[h].astype(F32) + local_ref[j, h]).astype(BF16)
            parts.append(factor * (qi_ref[rows, lanes] + dot(g_ref[rows, lanes], state, 1, 1)))
        out_ref[rows] = jnp.concatenate(parts, 1).astype(BF16).reshape(BLOCK, heads, depth)


def query_out(g, qi, local, far, factor):
    tokens, rows = g.shape
    heads, depth, _ = far.shape
    step = STEP
    wide = pl.BlockSpec((step, rows), lambda b: (b, 0))
    return pl.pallas_call(
        lambda *refs: query_kernel(heads, factor, *refs),
        grid=(tokens // step,),
        in_specs=[
            wide,
            wide,
            pl.BlockSpec((step // BLOCK, heads, depth, depth), lambda b: (b, 0, 0, 0)),
            pl.BlockSpec((heads, depth, depth), lambda b: (0, 0, 0)),
        ],
        out_specs=pl.BlockSpec((step, heads, depth), lambda b: (b, 0, 0)),
        out_shape=jax.ShapeDtypeStruct((tokens, heads, depth), BF16),
        compiler_params=params(12),
        name="query_out",
    )(g, qi, local, far)


def key_value_kernel(heads, factor, k_ref, v_ref, ki_ref, vi_ref, far_ref, ko_ref, vo_ref):
    depth = far_ref.shape[1]
    keys, values = [], []
    for h in range(heads):
        lanes = slice(h * depth, (h + 1) * depth)
        state = far_ref[h]
        keys.append(factor * (ki_ref[:, lanes].astype(F32) + dot(v_ref[h], state, 1, 1)))
        values.append(factor * (vi_ref[:, lanes].astype(F32) + dot(k_ref[h], state, 1, 0)))
    ko_ref[...] = jnp.concatenate(keys, 1).astype(BF16).reshape(ko_ref.shape)
    vo_ref[...] = jnp.concatenate(values, 1).astype(BF16).reshape(vo_ref.shape)


def key_value_out(k, v, ki, vi, far, factor, step=STEP):
    tokens, rows = ki.shape
    heads, depth, _ = far.shape
    split = pl.BlockSpec((heads, step, depth), lambda b: (0, b, 0))
    wide = pl.BlockSpec((step, rows), lambda b: (b, 0))
    out = pl.BlockSpec((step, heads, depth), lambda b: (b, 0, 0))
    return pl.pallas_call(
        lambda *refs: key_value_kernel(heads, factor, *refs),
        grid=(tokens // step,),
        in_specs=[
            split,
            split,
            wide,
            wide,
            pl.BlockSpec((heads, depth, depth), lambda b: (0, 0, 0)),
        ],
        out_specs=[out, out],
        out_shape=[jax.ShapeDtypeStruct((tokens, heads, depth), BF16)] * 2,
        compiler_params=params(18),
        name="key_value_out",
    )(k, v, ki, vi, far)


def body(queries, key_rows, value_rows, out_grad, out_weight):
    tokens, heads, depth = queries.shape
    shards = lax.axis_size("seq")
    columns = lax.axis_size("head")
    chips = columns // 2
    factor = 1.0 / math.sqrt(depth * tokens * shards)

    def along(shift):
        return [(2 * x + c, 2 * ((x + shift) % chips) + c) for x in range(chips) for c in range(2)]

    def send(array, pairs):
        return lax.ppermute(array, "head", pairs)

    swap = [(i, i ^ 1) for i in range(columns)]
    right, left = along(1), along(-1)
    half = tokens // 2

    w = out_weight.reshape(heads * depth, -1)

    from_left = send(out_grad, right)
    from_right = send(out_grad, left)

    k = key_rows.transpose(1, 0, 2)
    v = value_rows.transpose(1, 0, 2)

    kv_local, kv_total = kv_states(k, v)
    order = jnp.arange(shards)
    later = (order[:, None] < order[None, :]).astype(BF16)
    earlier = (order[:, None] > order[None, :]).astype(BF16)
    kv_total, k, v, later, earlier, queries = lax.optimization_barrier(
        (kv_total, k, v, later, earlier, queries)
    )
    rows = heads * depth // shards
    kv_pieces = lax.all_to_all(kv_total.reshape(shards, rows, depth), "seq", 0, 0, tiled=True)

    def scan(mask, pieces):
        sums = dot(mask, pieces.reshape(shards, rows * depth), 1, 0)
        return sums.astype(BF16).reshape(shards, rows, depth)

    kv_sums = scan(earlier, kv_pieces)
    from_left, from_right, kv_sums, queries, k, v, out_grad = lax.optimization_barrier(
        (from_left, from_right, kv_sums, queries, k, v, out_grad)
    )
    q = queries.transpose(1, 0, 2)
    to_right, to_left, near_left, near_right = lax.optimization_barrier(
        (from_left[:half], from_right[half:], from_left, from_right)
    )
    far_top = send(to_right, right)
    far_bottom = send(to_left, left)
    twin = send(out_grad, swap)
    from_left_twin = send(near_left, swap)
    from_right_twin = send(near_right, swap)
    acc = attn_add(
        None,
        [out_grad, twin, from_left, from_left_twin, from_right, from_right_twin],
        [(shift, other) for shift in (0, -1, 1) for other in (False, True)],
        w,
        "attn_near",
    )
    far_top, far_bottom, acc, q = lax.optimization_barrier((far_top, far_bottom, acc, q))
    far = jnp.concatenate([far_top, far_bottom], 0)
    far_twin = send(far, swap)
    acc = attn_add(acc, [far], [(2, False)], w, "attn_far")
    far_twin, acc = lax.optimization_barrier((far_twin, acc))
    grad, qg_local, qg_total = attn_last(far_twin, (2, True), w, acc, q)

    both = jnp.concatenate([qg_total.reshape(shards, rows, depth), kv_sums], 1)
    both = lax.all_to_all(both, "seq", 0, 0, tiled=True)
    qg_sums = scan(later, both[:, :rows])
    before = both[:, rows:].reshape(heads, depth, depth)
    after = lax.all_to_all(qg_sums, "seq", 0, 0, tiled=True).reshape(heads, depth, depth)

    qi, ki, vi = inner(q, k, v, grad, qg_local)
    ki, vi = in_hbm(ki), in_hbm(vi)
    query_grad = query_out(grad, qi, kv_local, before, factor)
    key_grad, value_grad = key_value_out(k, v, ki, vi, after, factor)
    return query_grad, key_grad, value_grad


def solution(mesh):
    placed = (
        P("seq", "head", None),
        P("seq", "head", None),
        P("seq", "head", None),
        P("seq", "head"),
        P("head", None, None),
    )
    return jax.shard_map(
        body,
        mesh=mesh,
        in_specs=placed,
        out_specs=(P("seq", "head", None), P("seq", "head", None), P("seq", "head", None)),
        check_vma=False,
    )
```
